32 devices in a mesh: events: 4 (over z), nodes: 8 (over y, x, core).
Axes of the slice: x: 2, y: 2, z: 4, core: 2. Of those that a mesh axis runs over, the one named last changes fastest.
Arguments:
- nodes_in: bfloat16 [4, 16384, 128], P('events', 'nodes'), may hold values from -6 to 6
- edge_latents: bfloat16 [4, 8, 8, 2, 128, 128], P('events', 'nodes'), may hold values from -6 to 6
- src_block: int32 [4, 8, 8, 2], P('events', 'nodes'), may hold values from 0 to 15
- src_offset: int32 [4, 8, 8, 2, 128], P('events', 'nodes'), may hold values from 0 to 127
- dst_block: int32 [4, 8, 8, 2], P('events', 'nodes'), may hold values from 0 to 15
- dst_offset: int32 [4, 8, 8, 2, 128], P('events', 'nodes'), may hold values from 0 to 127
- tile_counts: int32 [4, 8, 8], P('events'), may hold values from 1 to 2, as said below
- w_edge1: bfloat16 [384, 128], replicated, may hold values from -0.3125 to 0.3125
- b_edge1: float32 [128], replicated, may hold values from -3 to 3
- w_edge2: bfloat16 [128, 128], replicated, may hold values from -0.5 to 0.5
- b_edge2: float32 [128], replicated, may hold values from -3 to 3
- w_node1: bfloat16 [256, 128], replicated, may hold values from -0.375 to 0.375
- b_node1: float32 [128], replicated, may hold values from -3 to 3
- w_node2: bfloat16 [128, 128], replicated, may hold values from -0.5 to 0.5
- b_node2: float32 [128], replicated, may hold values from -3 to 3
- cotangent: bfloat16 [4, 16384, 128], P('events', 'nodes'), may hold values from -6 to 6
Outputs:
- new_nodes: bfloat16 [4, 16384, 128], P('events', 'nodes')
- node_grads: bfloat16 [4, 16384, 128], P('events', 'nodes')
- grad_w_edge1: float32 [384, 128], replicated
- grad_b_edge1: float32 [128], replicated
- grad_w_edge2: float32 [128, 128], replicated
- grad_b_edge2: float32 [128], replicated
- grad_w_node1: float32 [256, 128], replicated
- grad_b_node1: float32 [128], replicated
- grad_w_node2: float32 [128, 128], replicated
- grad_b_node2: float32 [128], replicated
The draws below stay inside these ranges and needn't reach their ends.
Inputs may be any that keep to these rules, and one draw needn't show every extreme that they name: tile_counts[g, s, d] is the number of live slots from source device s to destination device d; in every event group some destination device receives exactly 2 tiles from every source device.
All inputs are finite; a program needn't handle non-finite values.
Results may differ from the reference program's by a relative error of at most 0.0067.
Values may be sent and summed in bfloat16 or wider, within the bound.
A program may use at most 64 MiB of HBM per device.

```python
import jax
import jax.numpy as jnp

D = 128
H = 128
TILE = 128
CAP = 2
BLK_DEV = 16
GROUPS = 4
PEERS = 8
NODES = 16384


def draw_tile_counts(key, part):
    key_base = jax.random.fold_in(key, 11)
    key_full = jax.random.fold_in(key, 23)
    base = jax.random.randint(key_base, (GROUPS, PEERS, PEERS), 1, CAP // 2 + 1)
    full = jax.random.randint(key_full, (GROUPS, 1, 1), 0, PEERS)
    column = jnp.arange(PEERS, dtype=jnp.int32)[None, None, :]
    return jnp.where(column == full, CAP, base).astype(jnp.int32)


def with_ends(entries, stream_key, least, top_value):
    longest = entries.shape.index(max(entries.shape))
    spots = []
    for shift in (0, 1):
        where = [jax.random.randint(jax.random.fold_in(stream_key, axis), (), 0, length) for axis, length in enumerate(entries.shape)]
        where[longest] = (where[longest] + shift) % entries.shape[longest]
        spots.append(tuple(where))
    return entries.at[spots[0]].set(least).at[spots[1]].set(top_value)


def shard_levels(stream_key, dims, cuts, least, high):
    gain, own = 1.0, jax.random.fold_in(stream_key, 6)
    for dim, parts in cuts:
        steps = jnp.exp(jax.random.uniform(jax.random.fold_in(own, dim), (parts,), jnp.float32, least / len(cuts), high / len(cuts)))
        gain = gain * jnp.repeat(steps, dims[dim] // parts).reshape([-1 if axis == dim else 1 for axis in range(len(dims))])
    return gain


def scatter_about(own_key, dims, deviation, limit, shards=(), held_as=jnp.bfloat16):
    result = deviation * jax.random.normal(own_key, dims, jnp.float32)
    if shards:
        result = result * shard_levels(own_key, dims, shards, -0.22, 0.18)
    return jnp.clip(result, -limit, limit).astype(held_as)


def setup_inputs(seed: int = 0) -> dict:
    arg_keys = jax.random.split(jax.random.key(seed), 17)
    return {
        "nodes_in": scatter_about(arg_keys[0], (GROUPS, NODES, D), 1.0, 6.0, ((0, 4), (1, 8))),
        "edge_latents": scatter_about(arg_keys[1], (GROUPS, PEERS, PEERS, CAP, TILE, D), 1.0, 6.0, ((0, 4), (1, 8))),
        "src_block": with_ends(jax.random.randint(arg_keys[2], (GROUPS, PEERS, PEERS, CAP), 0, BLK_DEV), jax.random.fold_in(arg_keys[2], 1), 0, BLK_DEV - 1).astype(jnp.int32),
        "src_offset": with_ends(jax.random.randint(arg_keys[3], (GROUPS, PEERS, PEERS, CAP, TILE), 0, TILE), jax.random.fold_in(arg_keys[3], 1), 0, TILE - 1).astype(jnp.int32),
        "dst_block": with_ends(jax.random.randint(arg_keys[4], (GROUPS, PEERS, PEERS, CAP), 0, BLK_DEV), jax.random.fold_in(arg_keys[4], 1), 0, BLK_DEV - 1).astype(jnp.int32),
        "dst_offset": with_ends(jax.random.randint(arg_keys[5], (GROUPS, PEERS, PEERS, CAP, TILE), 0, TILE), jax.random.fold_in(arg_keys[5], 1), 0, TILE - 1).astype(jnp.int32),
        "tile_counts": draw_tile_counts(jax.random.fold_in(arg_keys[16], 71), 0),
        "w_edge1": scatter_about(arg_keys[7], (3 * D, H), (3 * D) ** -0.5, 0.3125),
        "b_edge1": scatter_about(arg_keys[8], (H,), 0.5, 3.0, (), jnp.float32),
        "w_edge2": scatter_about(arg_keys[9], (H, D), H ** -0.5, 0.5),
        "b_edge2": scatter_about(arg_keys[10], (D,), 0.5, 3.0, (), jnp.float32),
        "w_node1": scatter_about(arg_keys[11], (2 * D, H), (2 * D) ** -0.5, 0.375),
        "b_node1": scatter_about(arg_keys[12], (H,), 0.5, 3.0, (), jnp.float32),
        "w_node2": scatter_about(arg_keys[13], (H, D), H ** -0.5, 0.5),
        "b_node2": scatter_about(arg_keys[14], (D,), 0.5, 3.0, (), jnp.float32),
        "cotangent": scatter_about(arg_keys[15], (GROUPS, NODES, D), 1.0, 6.0, ((0, 4), (1, 8))),
    }


def silu_slope(value):
    sig = jax.nn.sigmoid(value)
    return sig * (1.0 + value * (1.0 - sig))


def reference(nodes_in, edge_latents, src_block, src_offset, dst_block, dst_offset, tile_counts, w_edge1, b_edge1, w_edge2, b_edge2, w_node1, b_node1, w_node2, b_node2, cotangent):
    node_dev = BLK_DEV * TILE
    total_nodes = node_dev * PEERS
    scale_factor = float(GROUPS * total_nodes) ** -0.5
    peer = jnp.arange(PEERS, dtype=jnp.int32)
    slot = jnp.arange(CAP, dtype=jnp.int32)
    w_src, w_dst, w_lat = w_edge1[:D], w_edge1[D:2 * D], w_edge1[2 * D:]
    w_own, w_agg = w_node1[:D], w_node1[D:]
    sums = [jnp.zeros((3 * D, H), jnp.float32), jnp.zeros((H,), jnp.float32), jnp.zeros((H, D), jnp.float32), jnp.zeros((D,), jnp.float32), jnp.zeros((2 * D, H), jnp.float32), jnp.zeros((H,), jnp.float32), jnp.zeros((H, D), jnp.float32), jnp.zeros((D,), jnp.float32)]
    news = []
    grads = []
    for group in range(GROUPS):
        nodes = nodes_in[group]
        cot = cotangent[group]
        src_rows = peer[:, None, None, None] * node_dev + src_block[group][..., None] * TILE + src_offset[group]
        src_rows = jnp.transpose(src_rows, (1, 0, 2, 3)).reshape(-1).astype(jnp.int32)
        dst_rows = (peer[:, None, None, None] * node_dev + dst_block[group][..., None] * TILE + dst_offset[group]).reshape(-1).astype(jnp.int32)
        counts = jnp.transpose(tile_counts[group])
        live = (slot[None, None, :] < counts[:, :, None])
        live = jnp.broadcast_to(live[..., None], (PEERS, PEERS, CAP, TILE)).reshape(-1, 1).astype(jnp.bfloat16)
        lat = edge_latents[group].reshape(-1, D)
        h_src = nodes[src_rows]
        h_dst = nodes[dst_rows]
        z_one = (jnp.dot(h_src, w_src, preferred_element_type=jnp.float32) + jnp.dot(h_dst, w_dst, preferred_element_type=jnp.float32) + jnp.dot(lat, w_lat, preferred_element_type=jnp.float32) + b_edge1)
        a_one = jax.nn.silu(z_one).astype(jnp.bfloat16)
        message = (jnp.dot(a_one, w_edge2, preferred_element_type=jnp.float32) + b_edge2).astype(jnp.bfloat16) * live
        agg = jax.ops.segment_sum(message.astype(jnp.float32), dst_rows, num_segments=total_nodes).astype(jnp.bfloat16)
        z_two = jnp.dot(nodes, w_own, preferred_element_type=jnp.float32) + jnp.dot(agg, w_agg, preferred_element_type=jnp.float32) + b_node1
        a_two = jax.nn.silu(z_two).astype(jnp.bfloat16)
        news.append((nodes.astype(jnp.float32) + jnp.dot(a_two, w_node2, preferred_element_type=jnp.float32) + b_node2).astype(jnp.bfloat16))
        g_two = (jnp.dot(cot, w_node2.T, preferred_element_type=jnp.float32) * silu_slope(z_two)).astype(jnp.bfloat16)
        g_agg = jnp.dot(g_two, w_agg.T, preferred_element_type=jnp.float32).astype(jnp.bfloat16)
        g_msg = g_agg[dst_rows] * live
        g_one = (jnp.dot(g_msg, w_edge2.T, preferred_element_type=jnp.float32) * silu_slope(z_one)).astype(jnp.bfloat16)
        g_src = jnp.dot(g_one, w_src.T, preferred_element_type=jnp.float32)
        g_dst = jnp.dot(g_one, w_dst.T, preferred_element_type=jnp.float32)
        total = cot.astype(jnp.float32) + jnp.dot(g_two, w_own.T, preferred_element_type=jnp.float32)
        total = total + jax.ops.segment_sum(g_dst, dst_rows, num_segments=total_nodes) + jax.ops.segment_sum(g_src, src_rows, num_segments=total_nodes)
        grads.append(total.astype(jnp.bfloat16))
        terms = [jnp.concatenate([jnp.dot(h_src.T, g_one, preferred_element_type=jnp.float32), jnp.dot(h_dst.T, g_one, preferred_element_type=jnp.float32), jnp.dot(lat.T, g_one, preferred_element_type=jnp.float32)], axis=0), jnp.sum(g_one.astype(jnp.float32), axis=0), jnp.dot(a_one.T, g_msg, preferred_element_type=jnp.float32), jnp.sum(g_msg.astype(jnp.float32), axis=0), jnp.concatenate([jnp.dot(nodes.T, g_two, preferred_element_type=jnp.float32), jnp.dot(agg.T, g_two, preferred_element_type=jnp.float32)], axis=0), jnp.sum(g_two.astype(jnp.float32), axis=0), jnp.dot(a_two.T, cot, preferred_element_type=jnp.float32), jnp.sum(cot.astype(jnp.float32), axis=0)]
        sums = [acc + term for acc, term in zip(sums, terms)]
    outs = [value * scale_factor for value in sums]
    return (jnp.stack(news), jnp.stack(grads), outs[0], outs[1], outs[2], outs[3], outs[4], outs[5], outs[6], outs[7])
```

```python
import functools

import jax
import jax.numpy as jnp
from jax import lax
from jax.experimental import pallas as pl
from jax.experimental.pallas import tpu as pltpu
from jax.sharding import PartitionSpec as P

F32 = jnp.float32
BF16 = jnp.bfloat16
MESH = pl.DeviceIdType.MESH


def dot(a, b):
    return jnp.dot(a, b, preferred_element_type=F32)


def dot_tl(a, b):
    return lax.dot_general(a, b, (((0,), (0,)), ((), ())), preferred_element_type=F32)


def dot_tr(a, b):
    return lax.dot_general(a, b, (((1,), (1,)), ((), ())), preferred_element_type=F32)


def act(v):
    s = jax.nn.sigmoid(v)
    return v * s, s * (1.0 + v * (1.0 - s))


def kernel(
    peers,
    zs,
    scale,
    nodes,
    lat,
    sblk,
    soff,
    dblk,
    doff,
    cnt,
    w1,
    b1,
    w2,
    b2,
    wn1,
    bn1,
    wn2,
    bn2,
    cot,
    upd,
    ngrad,
    gw1,
    gb1,
    gw2,
    gb2,
    gwn1,
    gbn1,
    gwn2,
    gbn2,
    hs,
    rh,
    ps,
    pd,
    hd,
    slope,
    a1,
    gm,
    g1,
    ret,
    st,
    st2,
    cw,
    agg,
    a2,
    g2,
    gag,
    sd,
    red,
    rbuf,
    zbuf,
    abuf,
    s_a,
    r_a,
    s_b,
    r_b,
    s_r,
    r_r,
    s_z,
    r_z,
    s_g,
    r_g,
):
    me = lax.axis_index("nodes")
    mz = lax.axis_index("events")
    slots, tile = soff.shape[3], soff.shape[4]
    nblk, width = nodes.shape[1], nodes.shape[3]
    rows = nblk * tile
    chunk = rbuf.shape[1]
    pair = slots * tile

    barrier = pltpu.get_barrier_semaphore()

    def greet(axis, mine, size):
        def body(i, c):
            pl.semaphore_signal(
                barrier, 1, device_id={axis: lax.rem(mine + i, size)}, device_id_type=MESH
            )
            return c

        lax.fori_loop(1, size, body, 0)

    greet("nodes", me, peers)
    greet("events", mz, zs)

    iota = lax.broadcasted_iota(jnp.int32, (tile, tile), 0)

    def onehot(off):
        return jnp.where(iota == off, 1.0, 0.0).astype(BF16)

    def copy(src, dst, s_sem, r_sem, axis, to):
        return pltpu.make_async_remote_copy(
            src_ref=src,
            dst_ref=dst,
            send_sem=s_sem,
            recv_sem=r_sem,
            device_id={axis: to},
            device_id_type=MESH,
        )

    def gather_src(p, into):
        for k in range(slots):
            hot = onehot(soff[0, 0, p, k : k + 1, :])
            ps[p, k] = hot
            block = nodes[0, sblk[0, 0, p, k]]
            into[p, k] = dot_tl(hot, block).astype(BF16)

    gather_src(me, rh)
    pl.semaphore_wait(barrier, peers - 1 + zs - 1)

    def copy_a(p):
        return copy(hs.at[p], rh.at[me], s_a.at[p], r_a.at[me], "nodes", p)

    def send_a(i, c):
        p = lax.rem(me + i, peers)
        gather_src(p, hs)
        copy_a(p).start()
        return c

    lax.fori_loop(1, peers, send_a, 0)

    def local(s, c):
        h = []
        for k in range(slots):
            live = jnp.minimum(jnp.maximum(cnt[0, s, me] - k, 0), 1)
            hot = onehot(doff[0, 0, s, k : k + 1, :] * live + (live - 1))
            pd[s, k] = hot
            block = nodes[0, dblk[0, 0, s, k]]
            h.append(dot_tl(hot, block).astype(BF16))
            hd[s, k] = h[k]
        x = jnp.concatenate(
            [jnp.concatenate(h, axis=0), lat[0, 0, s].reshape(pair, width)], axis=1
        )
        z = dot(x, w1[width:, :]) + b1[...]
        slope[s] = z.reshape(slots, tile, width)
        return c

    lax.fori_loop(0, peers, local, 0)

    cw[...] = dot_tr(cot[0], wn2[...])

    def forward(s):
        z = slope[s].reshape(pair, width) + dot(rh[s].reshape(pair, width), w1[:width, :])
        a, d = act(z)
        a = a.astype(BF16)
        slope[s] = d.reshape(slots, tile, width)
        a1[s] = a.reshape(slots, tile, width)
        msg = (dot(a, w2[...]) + b2[...]).astype(BF16)
        for k in range(slots):
            st[s, k] = dot(pd[s, k], msg[k * tile : (k + 1) * tile])

    forward(me)

    def recv_a(i, c):
        s = lax.rem(me + peers - i, peers)
        copy(hs.at[s], rh.at[s], s_a.at[s], r_a.at[s], "nodes", s).wait_recv()
        forward(s)
        return c

    lax.fori_loop(1, peers, recv_a, 0)

    def spread(parts, blocks, b):
        def body(s, acc):
            for k in range(slots):
                gap = blocks[0, 0, s, k] - b
                acc = acc + (1 - jnp.minimum(gap * gap, 1)).astype(F32) * parts[s, k]
            return acc

        return lax.fori_loop(
            0, peers, body, jnp.zeros((tile, width), F32), unroll=True if peers <= 8 else 8
        )

    group = 4 if nblk % 4 == 0 else 1
    span = group * tile

    def node(c, carry):
        at = pl.ds(pl.multiple_of(c * span, span), span)
        ag = jnp.concatenate(
            [spread(st, dblk, c * group + j).astype(BF16) for j in range(group)], axis=0
        )
        agg[at, :] = ag
        h = nodes[0, pl.ds(c * group, group)].reshape(span, width)
        z = dot(jnp.concatenate([h, ag], axis=1), wn1[...]) + bn1[...]
        a, d = act(z)
        a = a.astype(BF16)
        a2[at, :] = a
        upd[0, at, :] = (h.astype(F32) + dot(a, wn2[...]) + bn2[...]).astype(BF16)
        g = (cw[at, :] * d).astype(BF16)
        g2[at, :] = g
        gag[pl.ds(c * group, group)] = (
            dot_tr(g, wn1[width:, :]).astype(BF16).reshape(group, tile, width)
        )
        return carry

    lax.fori_loop(0, nblk // group, node, 0)

    def back(s):
        g = []
        for k in range(slots):
            block = gag[dblk[0, 0, s, k]]
            g.append(dot_tl(pd[s, k], block).astype(BF16))
            gm[s, k] = g[k]
        one = dot_tr(jnp.concatenate(g, axis=0), w2[...]) * slope[s].reshape(pair, width)
        return one.astype(BF16).reshape(slots, tile, width)

    def copy_b(p):
        return copy(g1.at[p], ret.at[me], s_b.at[p], r_b.at[me], "nodes", p)

    def send_b(i, c):
        p = lax.rem(me + i, peers)
        g1[p] = back(p)
        copy_b(p).start()
        return c

    lax.fori_loop(1, peers, send_b, 0)
    own = back(me)
    g1[me] = own
    ret[me] = own

    per = 8 if peers % 8 == 0 else peers
    span_e = per * pair

    def edges(c, carry):
        e1, e2, s1, s2 = carry
        at = pl.ds(c * per, per)
        g = g1[at].reshape(span_e, width)
        x = jnp.concatenate(
            [
                rh[at].reshape(span_e, width),
                hd[at].reshape(span_e, width),
                lat[0, 0, at].reshape(span_e, width),
            ],
            axis=1,
        )
        m = gm[at].reshape(span_e, width)
        e1 = e1 + dot_tl(g, x)
        e2 = e2 + dot_tl(a1[at].reshape(span_e, width), m)
        s1 = s1 + jnp.sum(g.astype(F32), axis=0, keepdims=True)
        s2 = s2 + jnp.sum(m.astype(F32), axis=0, keepdims=True)
        return e1, e2, s1, s2

    zero = jnp.zeros((1, width), F32)
    e1, e2, s1, s2 = lax.fori_loop(
        0,
        peers // per,
        edges,
        (jnp.zeros((width, 3 * width), F32), jnp.zeros((width, width), F32), zero, zero),
    )
    for j in range(3):
        red[j * width : (j + 1) * width, :] = e1[:, j * width : (j + 1) * width].T.astype(BF16)
    red[3 * width : 4 * width, :] = e2.astype(BF16)
    g = g2[...]
    n1 = dot_tl(g, jnp.concatenate([nodes[0].reshape(rows, width), agg[...]], axis=1))
    for j in range(2):
        red[(4 + j) * width : (5 + j) * width, :] = n1[:, j * width : (j + 1) * width].T.astype(
            BF16
        )
    red[6 * width : 7 * width, :] = dot_tl(a2[...], cot[0]).astype(BF16)
    s3 = jnp.sum(g.astype(F32), axis=0, keepdims=True)
    s4 = jnp.sum(cot[0].astype(F32), axis=0, keepdims=True)
    rest = red.shape[0] - 7 * width
    line = lax.broadcasted_iota(jnp.int32, (rest, width), 0)
    tail = jnp.zeros((rest, width), F32)
    for j, s in enumerate((s1, s2, s3, s4)):
        tail = jnp.where(line == j, s, tail)
    red[7 * width :, :] = tail.astype(BF16)

    def part(p):
        return pl.ds(pl.multiple_of(p * chunk, chunk), chunk)

    def copy_r(p):
        return copy(red.at[part(p), :], rbuf.at[me], s_r.at[p], r_r.at[me], "nodes", p)

    def send_r(i, c):
        copy_r(lax.rem(me + i, peers)).start()
        return c

    lax.fori_loop(1, peers, send_r, 0)
    rbuf[me] = red[part(me), :]

    def tiles_d(s, c):
        for k in range(slots):
            st[s, k] = dot(pd[s, k], g1[s, k])
        return c

    lax.fori_loop(0, peers, tiles_d, 0)

    def spread_d(b, c):
        sd[pl.ds(pl.multiple_of(b * tile, tile), tile), :] = spread(st, dblk, b).astype(BF16)
        return c

    lax.fori_loop(0, nblk, spread_d, 0)

    def recv_r(i, c):
        s = lax.rem(me + i, peers)
        copy(red.at[part(s), :], rbuf.at[s], s_r.at[s], r_r.at[s], "nodes", s).wait_recv()
        return c

    lax.fori_loop(1, peers, recv_r, 0)
    zbuf[mz] = jnp.sum(rbuf[...].astype(F32), axis=0).astype(BF16)

    def copy_z(p):
        return copy(zbuf.at[mz], zbuf.at[mz], s_z.at[p], r_z.at[mz], "events", p)

    def send_z(i, c):
        copy_z(lax.rem(mz + i, zs)).start()
        return c

    lax.fori_loop(1, zs, send_z, 0)

    def tiles_s(s):
        for k in range(slots):
            st2[s, k] = dot(ps[s, k], ret[s, k])

    tiles_s(me)

    def recv_b(i, c):
        s = lax.rem(me + peers - i, peers)
        copy(g1.at[s], ret.at[s], s_b.at[s], r_b.at[s], "nodes", s).wait_recv()
        tiles_s(s)
        return c

    lax.fori_loop(1, peers, recv_b, 0)

    def recv_z(i, c):
        s = lax.rem(mz + i, zs)
        copy(zbuf.at[s], zbuf.at[s], s_z.at[s], r_z.at[s], "events", s).wait_recv()
        return c

    lax.fori_loop(1, zs, recv_z, 0)
    abuf[me] = (jnp.sum(zbuf[...].astype(F32), axis=0) * scale).astype(BF16)

    def copy_g(p):
        return copy(abuf.at[me], abuf.at[me], s_g.at[p], r_g.at[me], "nodes", p)

    def send_g(i, c):
        copy_g(lax.rem(me + i, peers)).start()
        return c

    lax.fori_loop(1, peers, send_g, 0)

    def final(c, carry):
        at = pl.ds(pl.multiple_of(c * span, span), span)
        ss = jnp.concatenate(
            [spread(st2, sblk, c * group + j).astype(BF16) for j in range(group)], axis=0
        )
        total = (
            cot[0, at, :].astype(F32)
            + dot_tr(g2[at, :], wn1[:width, :])
            + dot_tr(sd[at, :], w1[width : 2 * width, :])
            + dot_tr(ss, w1[:width, :])
        )
        ngrad[0, at, :] = total.astype(BF16)
        return carry

    lax.fori_loop(0, nblk // group, final, 0)

    def recv_g(i, c):
        s = lax.rem(me + i, peers)
        copy(abuf.at[s], abuf.at[s], s_g.at[s], r_g.at[s], "nodes", s).wait_recv()
        return c

    lax.fori_loop(1, peers, recv_g, 0)
    full = abuf[...].reshape(peers * chunk, width)
    gw1[...] = full[: 3 * width].astype(F32)
    gw2[...] = full[3 * width : 4 * width].astype(F32)
    gwn1[...] = full[4 * width : 6 * width].astype(F32)
    gwn2[...] = full[6 * width : 7 * width].astype(F32)
    last = full[7 * width : 7 * width + 16].astype(F32)
    gb1[...] = last[0:1]
    gb2[...] = last[1:2]
    gbn1[...] = last[2:3]
    gbn2[...] = last[3:4]

    def drain(i, c):
        p = lax.rem(me + i, peers)
        copy_a(p).wait_send()
        copy_b(p).wait_send()
        copy_r(p).wait_send()
        copy_g(p).wait_send()
        return c

    lax.fori_loop(1, peers, drain, 0)

    def drain_z(i, c):
        copy_z(lax.rem(mz + i, zs)).wait_send()
        return c

    lax.fori_loop(1, zs, drain_z, 0)


def shards(
    peers,
    zs,
    nodes_in,
    edge_latents,
    src_block,
    src_offset,
    dst_block,
    dst_offset,
    tile_counts,
    w_edge1,
    b_edge1,
    w_edge2,
    b_edge2,
    w_node1,
    b_node1,
    w_node2,
    b_node2,
    cotangent,
):
    rows, width = nodes_in.shape[1:]
    slots, tile = src_offset.shape[3:]
    scale = float(zs * peers * rows) ** (-0.5)
    need = 7 * width + 16
    chunk = -(-need // (16 * peers)) * 16
    vec = lambda v: v.reshape(1, -1)
    vm = pl.BlockSpec(memory_space=pltpu.VMEM)
    sm = pl.BlockSpec(memory_space=pltpu.SMEM)
    tiles = (peers, slots, tile, width)
    sds = jax.ShapeDtypeStruct
    dma = pltpu.SemaphoreType.DMA
    outs = pl.pallas_call(
        functools.partial(kernel, peers, zs, scale),
        out_shape=(
            sds((1, rows, width), BF16),
            sds((1, rows, width), BF16),
            sds((3 * width, width), F32),
            sds((1, width), F32),
            sds((width, width), F32),
            sds((1, width), F32),
            sds((2 * width, width), F32),
            sds((1, width), F32),
            sds((width, width), F32),
            sds((1, width), F32),
        ),
        in_specs=[vm, vm, sm, vm, sm, vm, sm] + [vm] * 9,
        out_specs=(vm,) * 10,
        scratch_shapes=[
            pltpu.VMEM(tiles, BF16),
            pltpu.VMEM(tiles, BF16),
            pltpu.VMEM((peers, slots, tile, tile), BF16),
            pltpu.VMEM((peers, slots, tile, tile), BF16),
            pltpu.VMEM(tiles, BF16),
            pltpu.VMEM(tiles, F32),
            pltpu.VMEM(tiles, BF16),
            pltpu.VMEM(tiles, BF16),
            pltpu.VMEM(tiles, BF16),
            pltpu.VMEM(tiles, BF16),
            pltpu.VMEM(tiles, F32),
            pltpu.VMEM(tiles, F32),
            pltpu.VMEM((rows, width), F32),
            pltpu.VMEM((rows, width), BF16),
            pltpu.VMEM((rows, width), BF16),
            pltpu.VMEM((rows, width), BF16),
            pltpu.VMEM((rows // tile, tile, width), BF16),
            pltpu.VMEM((rows, width), BF16),
            pltpu.VMEM((peers * chunk, width), BF16),
            pltpu.VMEM((peers, chunk, width), BF16),
            pltpu.VMEM((zs, chunk, width), BF16),
            pltpu.VMEM((peers, chunk, width), BF16),
        ]
        + [dma((peers,))] * 6
        + [dma((zs,))] * 2
        + [dma((peers,))] * 2,
        compiler_params=pltpu.CompilerParams(
            collective_id=0, has_side_effects=True, vmem_limit_bytes=48 * 1024 * 1024
        ),
    )(
        nodes_in.reshape(1, rows // tile, tile, width),
        edge_latents,
        src_block,
        src_offset,
        dst_block,
        dst_offset,
        tile_counts,
        w_edge1,
        vec(b_edge1),
        w_edge2,
        vec(b_edge2),
        w_node1,
        vec(b_node1),
        w_node2,
        vec(b_node2),
        cotangent,
    )
    outs = list(outs)
    for j in (3, 5, 7, 9):
        outs[j] = outs[j].reshape(-1)
    return tuple(outs)


def solution(mesh):
    return jax.shard_map(
        functools.partial(shards, mesh.shape["nodes"], mesh.shape["events"]),
        mesh=mesh,
        in_specs=(
            P("events", "nodes", None),
            P("events", "nodes", None, None, None, None),
            P("events", "nodes", None, None),
            P("events", "nodes", None, None, None),
            P("events", "nodes", None, None),
            P("events", "nodes", None, None, None),
            P("events", None, None),
            P(),
            P(),
            P(),
            P(),
            P(),
            P(),
            P(),
            P(),
            P("events", "nodes", None),
        ),
        out_specs=(
            P("events", "nodes", None),
            P("events", "nodes", None),
            P(),
            P(),
            P(),
            P(),
            P(),
            P(),
            P(),
            P(),
        ),
        check_vma=False,
    )
```

```python
import functools

import jax
import jax.numpy as jnp
from jax import lax
from jax.experimental import pallas as pl
from jax.experimental.pallas import tpu as pltpu
from jax.sharding import PartitionSpec as P

F32 = jnp.float32
BF16 = jnp.bfloat16
MESH = pl.DeviceIdType.MESH


def dot(a, b):
    return jnp.dot(a, b, preferred_element_type=F32)


def dot_tl(a, b):
    return lax.dot_general(a, b, (((0,), (0,)), ((), ())), preferred_element_type=F32)


def dot_tr(a, b):
    return lax.dot_general(a, b, (((1,), (1,)), ((), ())), preferred_element_type=F32)


def act(v):
    s = jax.nn.sigmoid(v)
    return v * s, s * (1.0 + v * (1.0 - s))


def staged(peers, zs, scale, held, *refs):
    ins, rest = list(refs[:16]), list(refs[16:])
    sems = rest.pop()
    local, rest = rest[-len(held) :], rest[: -len(held)]
    copies = {}
    for n, j in enumerate(held):
        copies[j] = pltpu.make_async_copy(ins[j], local[n], sems.at[n])
        copies[j].start()
        ins[j] = local[n]
    kernel(peers, zs, scale, copies, *ins, *rest)


def kernel(
    peers,
    zs,
    scale,
    copies,
    nodes,
    lat,
    sblk,
    soff,
    dblk,
    doff,
    cnt,
    w1,
    b1,
    w2,
    b2,
    wn1,
    bn1,
    wn2,
    bn2,
    cot,
    upd,
    ngrad,
    gw1,
    gb1,
    gw2,
    gb2,
    gwn1,
    gbn1,
    gwn2,
    gbn2,
    hs,
    rh,
    ps,
    pd,
    hd,
    slope,
    a1,
    gm,
    g1,
    ret,
    st,
    st2,
    cw,
    agg,
    a2,
    g2,
    gag,
    sd,
    red,
    rbuf,
    zbuf,
    abuf,
    s_a,
    r_a,
    s_b,
    r_b,
    s_r,
    r_r,
    s_z,
    r_z,
    s_g,
    r_g,
):
    me = lax.axis_index("nodes")
    mz = lax.axis_index("events")
    slots, tile = soff.shape[3], soff.shape[4]
    nblk, width = nodes.shape[1], nodes.shape[3]
    rows = nblk * tile
    chunk = rbuf.shape[1]
    pair = slots * tile

    barrier = pltpu.get_barrier_semaphore()

    def greet(axis, mine, size):
        def body(i, c):
            pl.semaphore_signal(
                barrier, 1, device_id={axis: lax.rem(mine + i, size)}, device_id_type=MESH
            )
            return c

        lax.fori_loop(1, size, body, 0)

    greet("nodes", me, peers)
    greet("events", mz, zs)

    iota = lax.broadcasted_iota(jnp.int32, (tile, tile), 0)

    def onehot(off):
        return jnp.where(iota == off, 1.0, 0.0).astype(BF16)

    def copy(src, dst, s_sem, r_sem, axis, to):
        return pltpu.make_async_remote_copy(
            src_ref=src,
            dst_ref=dst,
            send_sem=s_sem,
            recv_sem=r_sem,
            device_id={axis: to},
            device_id_type=MESH,
        )

    def gather_src(p, into):
        for k in range(slots):
            hot = onehot(soff[0, 0, p, k : k + 1, :])
            ps[p, k] = hot
            block = nodes[0, sblk[0, 0, p, k]]
            into[p, k] = dot_tl(hot, block).astype(BF16)

    for j in (0, 3):
        copies[j].wait()
    gather_src(me, rh)
    pl.semaphore_wait(barrier, peers - 1 + zs - 1)

    def copy_a(p):
        return copy(hs.at[p], rh.at[me], s_a.at[p], r_a.at[me], "nodes", p)

    def send_a(i, c):
        p = lax.rem(me + i, peers)
        gather_src(p, hs)
        copy_a(p).start()
        return c

    lax.fori_loop(1, peers, send_a, 0)

    for j in copies:
        if j not in (0, 3):
            copies[j].wait()

    def local(s, c):
        h = []
        for k in range(slots):
            live = jnp.minimum(jnp.maximum(cnt[0, s, me] - k, 0), 1)
            hot = onehot(doff[0, 0, s, k : k + 1, :] * live + (live - 1))
            pd[s, k] = hot
            block = nodes[0, dblk[0, 0, s, k]]
            h.append(dot_tl(hot, block).astype(BF16))
            hd[s, k] = h[k]
        x = jnp.concatenate(
            [jnp.concatenate(h, axis=0), lat[0, 0, s].reshape(pair, width)], axis=1
        )
        z = dot(x, w1[width:, :]) + b1[...]
        slope[s] = z.reshape(slots, tile, width)
        return c

    lax.fori_loop(0, peers, local, 0, unroll=4)

    cw[...] = dot_tr(cot[0], wn2[...])

    def forward(s):
        z = slope[s].reshape(pair, width) + dot(rh[s].reshape(pair, width), w1[:width, :])
        a, d = act(z)
        a = a.astype(BF16)
        slope[s] = d.reshape(slots, tile, width)
        a1[s] = a.reshape(slots, tile, width)
        msg = (dot(a, w2[...]) + b2[...]).astype(BF16)
        for k in range(slots):
            st[s, k] = dot(pd[s, k], msg[k * tile : (k + 1) * tile])

    forward(me)

    def recv_a(i, c):
        s = lax.rem(me + peers - i, peers)
        copy(hs.at[s], rh.at[s], s_a.at[s], r_a.at[s], "nodes", s).wait_recv()
        forward(s)
        return c

    lax.fori_loop(1, peers, recv_a, 0)

    def spread(parts, blocks, b):
        def body(s, acc):
            for k in range(slots):
                gap = blocks[0, 0, s, k] - b
                acc = acc + (1 - jnp.minimum(gap * gap, 1)).astype(F32) * parts[s, k]
            return acc

        return lax.fori_loop(
            0, peers, body, jnp.zeros((tile, width), F32), unroll=True if peers <= 8 else 8
        )

    group = 4 if nblk % 4 == 0 else 1
    span = group * tile

    def node(c, carry):
        at = pl.ds(pl.multiple_of(c * span, span), span)
        ag = jnp.concatenate(
            [spread(st, dblk, c * group + j).astype(BF16) for j in range(group)], axis=0
        )
        agg[at, :] = ag
        h = nodes[0, pl.ds(c * group, group)].reshape(span, width)
        z = dot(jnp.concatenate([h, ag], axis=1), wn1[...]) + bn1[...]
        a, d = act(z)
        a = a.astype(BF16)
        a2[at, :] = a
        upd[0, at, :] = (h.astype(F32) + dot(a, wn2[...]) + bn2[...]).astype(BF16)
        g = (cw[at, :] * d).astype(BF16)
        g2[at, :] = g
        gag[pl.ds(c * group, group)] = (
            dot_tr(g, wn1[width:, :]).astype(BF16).reshape(group, tile, width)
        )
        return carry

    lax.fori_loop(0, nblk // group, node, 0)

    def back(s):
        g = []
        for k in range(slots):
            block = gag[dblk[0, 0, s, k]]
            g.append(dot_tl(pd[s, k], block).astype(BF16))
            gm[s, k] = g[k]
        one = dot_tr(jnp.concatenate(g, axis=0), w2[...]) * slope[s].reshape(pair, width)
        return one.astype(BF16).reshape(slots, tile, width)

    def copy_b(p):
        return copy(g1.at[p], ret.at[me], s_b.at[p], r_b.at[me], "nodes", p)

    def send_b(i, c):
        p = lax.rem(me + i, peers)
        g1[p] = back(p)
        copy_b(p).start()
        return c

    lax.fori_loop(1, peers, send_b, 0)
    own = back(me)
    g1[me] = own
    ret[me] = own

    per = 8 if peers % 8 == 0 else peers
    span_e = per * pair

    def edges(c, carry):
        e1, e2, s1, s2 = carry
        at = pl.ds(c * per, per)
        g = g1[at].reshape(span_e, width)
        x = jnp.concatenate(
            [
                rh[at].reshape(span_e, width),
                hd[at].reshape(span_e, width),
                lat[0, 0, at].reshape(span_e, width),
            ],
            axis=1,
        )
        m = gm[at].reshape(span_e, width)
        e1 = e1 + dot_tl(g, x)
        e2 = e2 + dot_tl(a1[at].reshape(span_e, width), m)
        s1 = s1 + jnp.sum(g.astype(F32), axis=0, keepdims=True)
        s2 = s2 + jnp.sum(m.astype(F32), axis=0, keepdims=True)
        return e1, e2, s1, s2

    zero = jnp.zeros((1, width), F32)
    e1, e2, s1, s2 = lax.fori_loop(
        0,
        peers // per,
        edges,
        (jnp.zeros((width, 3 * width), F32), jnp.zeros((width, width), F32), zero, zero),
    )
    for j in range(3):
        red[j * width : (j + 1) * width, :] = e1[:, j * width : (j + 1) * width].T.astype(BF16)
    red[3 * width : 4 * width, :] = e2.astype(BF16)
    g = g2[...]
    n1 = dot_tl(g, jnp.concatenate([nodes[0].reshape(rows, width), agg[...]], axis=1))
    for j in range(2):
        red[(4 + j) * width : (5 + j) * width, :] = n1[:, j * width : (j + 1) * width].T.astype(
            BF16
        )
    red[6 * width : 7 * width, :] = dot_tl(a2[...], cot[0]).astype(BF16)
    s3 = jnp.sum(g.astype(F32), axis=0, keepdims=True)
    s4 = jnp.sum(cot[0].astype(F32), axis=0, keepdims=True)
    rest = red.shape[0] - 7 * width
    line = lax.broadcasted_iota(jnp.int32, (rest, width), 0)
    tail = jnp.zeros((rest, width), F32)
    for j, s in enumerate((s1, s2, s3, s4)):
        tail = jnp.where(line == j, s, tail)
    red[7 * width :, :] = tail.astype(BF16)

    def part(p):
        return pl.ds(pl.multiple_of(p * chunk, chunk), chunk)

    def copy_r(p):
        return copy(red.at[part(p), :], rbuf.at[me], s_r.at[p], r_r.at[me], "nodes", p)

    def send_r(i, c):
        copy_r(lax.rem(me + i, peers)).start()
        return c

    lax.fori_loop(1, peers, send_r, 0)
    rbuf[me] = red[part(me), :]

    def tiles_d(s, c):
        for k in range(slots):
            st[s, k] = dot(pd[s, k], g1[s, k])
        return c

    lax.fori_loop(0, peers, tiles_d, 0, unroll=4)

    def spread_d(b, c):
        sd[pl.ds(pl.multiple_of(b * tile, tile), tile), :] = spread(st, dblk, b).astype(BF16)
        return c

    lax.fori_loop(0, nblk, spread_d, 0)

    def recv_r(i, c):
        s = lax.rem(me + i, peers)
        copy(red.at[part(s), :], rbuf.at[s], s_r.at[s], r_r.at[s], "nodes", s).wait_recv()
        return c

    lax.fori_loop(1, peers, recv_r, 0)
    zbuf[mz] = jnp.sum(rbuf[...].astype(F32), axis=0).astype(BF16)

    def copy_z(p):
        return copy(zbuf.at[mz], zbuf.at[mz], s_z.at[p], r_z.at[mz], "events", p)

    def send_z(i, c):
        copy_z(lax.rem(mz + i, zs)).start()
        return c

    lax.fori_loop(1, zs, send_z, 0)

    def tiles_s(s):
        for k in range(slots):
            st2[s, k] = dot(ps[s, k], ret[s, k])

    tiles_s(me)

    def recv_b(i, c):
        s = lax.rem(me + peers - i, peers)
        copy(g1.at[s], ret.at[s], s_b.at[s], r_b.at[s], "nodes", s).wait_recv()
        tiles_s(s)
        return c

    lax.fori_loop(1, peers, recv_b, 0)

    def recv_z(i, c):
        s = lax.rem(mz + i, zs)
        copy(zbuf.at[s], zbuf.at[s], s_z.at[s], r_z.at[s], "events", s).wait_recv()
        return c

    lax.fori_loop(1, zs, recv_z, 0)
    abuf[me] = (jnp.sum(zbuf[...].astype(F32), axis=0) * scale).astype(BF16)

    def copy_g(p):
        return copy(abuf.at[me], abuf.at[me], s_g.at[p], r_g.at[me], "nodes", p)

    def send_g(i, c):
        copy_g(lax.rem(me + i, peers)).start()
        return c

    lax.fori_loop(1, peers, send_g, 0)

    def final(c, carry):
        at = pl.ds(pl.multiple_of(c * span, span), span)
        ss = jnp.concatenate(
            [spread(st2, sblk, c * group + j).astype(BF16) for j in range(group)], axis=0
        )
        total = (
            cot[0, at, :].astype(F32)
            + dot_tr(g2[at, :], wn1[:width, :])
            + dot_tr(sd[at, :], w1[width : 2 * width, :])
            + dot_tr(ss, w1[:width, :])
        )
        ngrad[0, at, :] = total.astype(BF16)
        return carry

    lax.fori_loop(0, nblk // group, final, 0)

    def recv_g(i, c):
        s = lax.rem(me + i, peers)
        copy(abuf.at[s], abuf.at[s], s_g.at[s], r_g.at[s], "nodes", s).wait_recv()
        return c

    lax.fori_loop(1, peers, recv_g, 0)
    full = abuf[...].reshape(peers * chunk, width)
    gw1[...] = full[: 3 * width].astype(F32)
    gw2[...] = full[3 * width : 4 * width].astype(F32)
    gwn1[...] = full[4 * width : 6 * width].astype(F32)
    gwn2[...] = full[6 * width : 7 * width].astype(F32)
    last = full[7 * width : 7 * width + 16].astype(F32)
    gb1[...] = last[0:1]
    gb2[...] = last[1:2]
    gbn1[...] = last[2:3]
    gbn2[...] = last[3:4]

    def drain(i, c):
        p = lax.rem(me + i, peers)
        copy_a(p).wait_send()
        copy_b(p).wait_send()
        copy_r(p).wait_send()
        copy_g(p).wait_send()
        return c

    lax.fori_loop(1, peers, drain, 0)

    def drain_z(i, c):
        copy_z(lax.rem(mz + i, zs)).wait_send()
        return c

    lax.fori_loop(1, zs, drain_z, 0)


def shards(
    peers,
    zs,
    nodes_in,
    edge_latents,
    src_block,
    src_offset,
    dst_block,
    dst_offset,
    tile_counts,
    w_edge1,
    b_edge1,
    w_edge2,
    b_edge2,
    w_node1,
    b_node1,
    w_node2,
    b_node2,
    cotangent,
):
    rows, width = nodes_in.shape[1:]
    slots, tile = src_offset.shape[3:]
    scale = float(zs * peers * rows) ** (-0.5)
    need = 7 * width + 16
    chunk = -(-need // (16 * peers)) * 16
    vec = lambda v: v.reshape(1, -1)
    vm = pl.BlockSpec(memory_space=pltpu.VMEM)
    hbm = pl.BlockSpec(memory_space=pl.ANY)
    sm = pl.BlockSpec(memory_space=pltpu.SMEM)
    tiles = (peers, slots, tile, width)
    sds = jax.ShapeDtypeStruct
    dma = pltpu.SemaphoreType.DMA
    args = (
        nodes_in.reshape(1, rows // tile, tile, width),
        edge_latents,
        src_block,
        src_offset,
        dst_block,
        dst_offset,
        tile_counts,
        w_edge1,
        vec(b_edge1),
        w_edge2,
        vec(b_edge2),
        w_node1,
        vec(b_node1),
        w_node2,
        vec(b_node2),
        cotangent,
    )
    held = (3, 0, 5, 1, 7, 8, 15, 9, 10, 11, 12, 13, 14)
    outs = pl.pallas_call(
        functools.partial(staged, peers, zs, scale, held),
        out_shape=(
            sds((1, rows, width), BF16),
            sds((1, rows, width), BF16),
            sds((3 * width, width), F32),
            sds((1, width), F32),
            sds((width, width), F32),
            sds((1, width), F32),
            sds((2 * width, width), F32),
            sds((1, width), F32),
            sds((width, width), F32),
            sds((1, width), F32),
        ),
        in_specs=[sm if j in (2, 4, 6) else hbm for j in range(16)],
        out_specs=(vm,) * 10,
        scratch_shapes=[
            pltpu.VMEM(tiles, BF16),
            pltpu.VMEM(tiles, BF16),
            pltpu.VMEM((peers, slots, tile, tile), BF16),
            pltpu.VMEM((peers, slots, tile, tile), BF16),
            pltpu.VMEM(tiles, BF16),
            pltpu.VMEM(tiles, F32),
            pltpu.VMEM(tiles, BF16),
            pltpu.VMEM(tiles, BF16),
            pltpu.VMEM(tiles, BF16),
            pltpu.VMEM(tiles, BF16),
            pltpu.VMEM(tiles, F32),
            pltpu.VMEM(tiles, F32),
            pltpu.VMEM((rows, width), F32),
            pltpu.VMEM((rows, width), BF16),
            pltpu.VMEM((rows, width), BF16),
            pltpu.VMEM((rows, width), BF16),
            pltpu.VMEM((rows // tile, tile, width), BF16),
            pltpu.VMEM((rows, width), BF16),
            pltpu.VMEM((peers * chunk, width), BF16),
            pltpu.VMEM((peers, chunk, width), BF16),
            pltpu.VMEM((zs, chunk, width), BF16),
            pltpu.VMEM((peers, chunk, width), BF16),
        ]
        + [dma((peers,))] * 6
        + [dma((zs,))] * 2
        + [dma((peers,))] * 2
        + [pltpu.VMEM(args[j].shape, args[j].dtype) for j in held]
        + [dma((len(held),))],
        compiler_params=pltpu.CompilerParams(
            collective_id=0, has_side_effects=True, vmem_limit_bytes=56 * 1024 * 1024
        ),
    )(*args)
    outs = list(outs)
    for j in (3, 5, 7, 9):
        outs[j] = outs[j].reshape(-1)
    return tuple(outs)


def solution(mesh):
    return jax.shard_map(
        functools.partial(shards, mesh.shape["nodes"], mesh.shape["events"]),
        mesh=mesh,
        in_specs=(
            P("events", "nodes", None),
            P("events", "nodes", None, None, None, None),
            P("events", "nodes", None, None),
            P("events", "nodes", None, None, None),
            P("events", "nodes", None, None),
            P("events", "nodes", None, None, None),
            P("events", None, None),
            P(),
            P(),
            P(),
            P(),
            P(),
            P(),
            P(),
            P(),
            P("events", "nodes", None),
        ),
        out_specs=(
            P("events", "nodes", None),
            P("events", "nodes", None),
            P(),
            P(),
            P(),
            P(),
            P(),
            P(),
            P(),
            P(),
        ),
        check_vma=False,
    )
```

```python
import functools

import jax
import jax.numpy as jnp
from jax import lax
from jax.experimental import pallas as pl
from jax.experimental.pallas import tpu as pltpu
from jax.sharding import PartitionSpec as P

F32 = jnp.float32
BF16 = jnp.bfloat16
MESH = pl.DeviceIdType.MESH


def dot(a, b):
    return jnp.dot(a, b, preferred_element_type=F32)


def dot_tl(a, b):
    return lax.dot_general(a, b, (((0,), (0,)), ((), ())), preferred_element_type=F32)


def dot_tr(a, b):
    return lax.dot_general(a, b, (((1,), (1,)), ((), ())), preferred_element_type=F32)


def act(v):
    s = jax.nn.sigmoid(v)
    return v * s, s * (1.0 + v * (1.0 - s))


def staged(peers, zs, scale, held, *refs):
    ins, rest = list(refs[:16]), list(refs[16:])
    sems = rest.pop()
    local, rest = rest[-len(held) :], rest[: -len(held)]
    copies = {}
    for n, j in enumerate(held):
        copies[j] = pltpu.make_async_copy(ins[j], local[n], sems.at[n])
        copies[j].start()
        ins[j] = local[n]
    kernel(peers, zs, scale, copies, *ins, *rest)


def kernel(
    peers,
    zs,
    scale,
    copies,
    nodes,
    lat,
    sblk,
    soff,
    dblk,
    doff,
    cnt,
    w1,
    b1,
    w2,
    b2,
    wn1,
    bn1,
    wn2,
    bn2,
    cot,
    upd,
    ngrad,
    grads,
    hs,
    rh,
    ps,
    pd,
    hd,
    slope,
    a1,
    gm,
    g1,
    ret,
    st,
    st2,
    cw,
    agg,
    a2,
    g2,
    gag,
    sd,
    red,
    rbuf,
    zbuf,
    abuf,
    s_a,
    r_a,
    s_b,
    r_b,
    s_r,
    r_r,
    s_z,
    r_z,
    s_g,
    r_g,
):
    me = lax.axis_index("nodes")
    mz = lax.axis_index("events")
    slots, tile = soff.shape[3], soff.shape[4]
    nblk, width = nodes.shape[1], nodes.shape[3]
    rows = nblk * tile
    chunk = rbuf.shape[1]
    pair = slots * tile

    barrier = pltpu.get_barrier_semaphore()

    def greet(axis, mine, size):
        def body(i, c):
            pl.semaphore_signal(
                barrier, 1, device_id={axis: lax.rem(mine + i, size)}, device_id_type=MESH
            )
            return c

        lax.fori_loop(1, size, body, 0)

    greet("nodes", me, peers)
    greet("events", mz, zs)

    iota = lax.broadcasted_iota(jnp.int32, (tile, tile), 0)

    def onehot(off):
        return jnp.where(iota == off, 1.0, 0.0).astype(BF16)

    def copy(src, dst, s_sem, r_sem, axis, to):
        return pltpu.make_async_remote_copy(
            src_ref=src,
            dst_ref=dst,
            send_sem=s_sem,
            recv_sem=r_sem,
            device_id={axis: to},
            device_id_type=MESH,
        )

    def gather_src(p, into):
        for k in range(slots):
            hot = onehot(soff[0, 0, p, k : k + 1, :])
            ps[p, k] = hot
            block = nodes[0, sblk[0, 0, p, k]]
            into[p, k] = dot_tl(hot, block).astype(BF16)

    for j in (0, 3):
        copies[j].wait()
    gather_src(me, rh)
    pl.semaphore_wait(barrier, peers - 1 + zs - 1)

    def copy_a(p):
        return copy(hs.at[p], rh.at[me], s_a.at[p], r_a.at[me], "nodes", p)

    def send_a(i, c):
        p = lax.rem(me + i, peers)
        gather_src(p, hs)
        copy_a(p).start()
        return c

    lax.fori_loop(1, peers, send_a, 0)

    for j in copies:
        if j not in (0, 3):
            copies[j].wait()

    def local(s, c):
        h = []
        for k in range(slots):
            live = jnp.minimum(jnp.maximum(cnt[0, s, me] - k, 0), 1)
            hot = onehot(doff[0, 0, s, k : k + 1, :] * live + (live - 1))
            pd[s, k] = hot
            block = nodes[0, dblk[0, 0, s, k]]
            h.append(dot_tl(hot, block).astype(BF16))
            hd[s, k] = h[k]
        x = jnp.concatenate(
            [jnp.concatenate(h, axis=0), lat[0, 0, s].reshape(pair, width)], axis=1
        )
        z = dot(x, w1[width:, :]) + b1[...]
        slope[s] = z.reshape(slots, tile, width)
        return c

    lax.fori_loop(0, peers, local, 0, unroll=4)

    cw[...] = dot_tr(cot[0], wn2[...])

    def forward(s):
        z = slope[s].reshape(pair, width) + dot(rh[s].reshape(pair, width), w1[:width, :])
        a, d = act(z)
        a = a.astype(BF16)
        slope[s] = d.reshape(slots, tile, width)
        a1[s] = a.reshape(slots, tile, width)
        msg = (dot(a, w2[...]) + b2[...]).astype(BF16)
        for k in range(slots):
            st[s, k] = dot(pd[s, k], msg[k * tile : (k + 1) * tile])

    forward(me)

    def recv_a(i, c):
        s = lax.rem(me + peers - i, peers)
        copy(hs.at[s], rh.at[s], s_a.at[s], r_a.at[s], "nodes", s).wait_recv()
        forward(s)
        return c

    lax.fori_loop(1, peers, recv_a, 0)

    def spread(parts, blocks, b):
        def body(s, acc):
            for k in range(slots):
                gap = blocks[0, 0, s, k] - b
                acc = acc + (1 - jnp.minimum(gap * gap, 1)).astype(F32) * parts[s, k]
            return acc

        return lax.fori_loop(
            0, peers, body, jnp.zeros((tile, width), F32), unroll=True if peers <= 8 else 8
        )

    group = 8 if nblk % 8 == 0 else 1
    span = group * tile

    def node(c, carry):
        at = pl.ds(pl.multiple_of(c * span, span), span)
        ag = jnp.concatenate(
            [spread(st, dblk, c * group + j).astype(BF16) for j in range(group)], axis=0
        )
        agg[at, :] = ag
        h = nodes[0, pl.ds(c * group, group)].reshape(span, width)
        z = dot(jnp.concatenate([h, ag], axis=1), wn1[...]) + bn1[...]
        a, d = act(z)
        a = a.astype(BF16)
        a2[at, :] = a
        upd[0, at, :] = (h.astype(F32) + dot(a, wn2[...]) + bn2[...]).astype(BF16)
        g = (cw[at, :] * d).astype(BF16)
        g2[at, :] = g
        gag[pl.ds(c * group, group)] = (
            dot_tr(g, wn1[width:, :]).astype(BF16).reshape(group, tile, width)
        )
        return carry

    lax.fori_loop(0, nblk // group, node, 0)

    def back(s):
        g = []
        for k in range(slots):
            block = gag[dblk[0, 0, s, k]]
            g.append(dot_tl(pd[s, k], block).astype(BF16))
            gm[s, k] = g[k]
        one = dot_tr(jnp.concatenate(g, axis=0), w2[...]) * slope[s].reshape(pair, width)
        return one.astype(BF16).reshape(slots, tile, width)

    def copy_b(p):
        return copy(g1.at[p], ret.at[me], s_b.at[p], r_b.at[me], "nodes", p)

    def send_b(i, c):
        p = lax.rem(me + i, peers)
        g1[p] = back(p)
        copy_b(p).start()
        return c

    lax.fori_loop(1, peers, send_b, 0)
    own = back(me)
    g1[me] = own
    ret[me] = own

    per = 8 if peers % 8 == 0 else peers
    span_e = per * pair

    def edges(c, carry):
        e1, e2, s1, s2 = carry
        at = pl.ds(c * per, per)
        g = g1[at].reshape(span_e, width)
        x = jnp.concatenate(
            [
                rh[at].reshape(span_e, width),
                hd[at].reshape(span_e, width),
                lat[0, 0, at].reshape(span_e, width),
            ],
            axis=1,
        )
        m = gm[at].reshape(span_e, width)
        e1 = e1 + dot_tl(g, x)
        e2 = e2 + dot_tl(a1[at].reshape(span_e, width), m)
        s1 = s1 + jnp.sum(g.astype(F32), axis=0, keepdims=True)
        s2 = s2 + jnp.sum(m.astype(F32), axis=0, keepdims=True)
        return e1, e2, s1, s2

    zero = jnp.zeros((1, width), F32)
    e1, e2, s1, s2 = lax.fori_loop(
        0,
        peers // per,
        edges,
        (jnp.zeros((width, 3 * width), F32), jnp.zeros((width, width), F32), zero, zero),
    )
    for j in range(3):
        red[j * width : (j + 1) * width, :] = e1[:, j * width : (j + 1) * width].T.astype(BF16)
    red[3 * width : 4 * width, :] = e2.astype(BF16)
    g = g2[...]
    n1 = dot_tl(g, jnp.concatenate([nodes[0].reshape(rows, width), agg[...]], axis=1))
    for j in range(2):
        red[(4 + j) * width : (5 + j) * width, :] = n1[:, j * width : (j + 1) * width].T.astype(
            BF16
        )
    red[6 * width : 7 * width, :] = dot_tl(a2[...], cot[0]).astype(BF16)
    s3 = jnp.sum(g.astype(F32), axis=0, keepdims=True)
    s4 = jnp.sum(cot[0].astype(F32), axis=0, keepdims=True)
    rest = red.shape[0] - 7 * width
    line = lax.broadcasted_iota(jnp.int32, (rest, width), 0)
    tail = jnp.zeros((rest, width), F32)
    for j, s in enumerate((s1, s2, s3, s4)):
        tail = jnp.where(line == j, s, tail)
    red[7 * width :, :] = tail.astype(BF16)

    def part(p):
        return pl.ds(pl.multiple_of(p * chunk, chunk), chunk)

    def copy_r(p):
        return copy(red.at[part(p), :], rbuf.at[me], s_r.at[p], r_r.at[me], "nodes", p)

    def send_r(i, c):
        copy_r(lax.rem(me + i, peers)).start()
        return c

    lax.fori_loop(1, peers, send_r, 0)
    rbuf[me] = red[part(me), :]

    def tiles_d(s, c):
        for k in range(slots):
            st[s, k] = dot(pd[s, k], g1[s, k])
        return c

    lax.fori_loop(0, peers, tiles_d, 0, unroll=4)

    def spread_d(b, c):
        sd[pl.ds(pl.multiple_of(b * tile, tile), tile), :] = spread(st, dblk, b).astype(BF16)
        return c

    lax.fori_loop(0, nblk, spread_d, 0)

    def recv_r(i, c):
        s = lax.rem(me + i, peers)
        copy(red.at[part(s), :], rbuf.at[s], s_r.at[s], r_r.at[s], "nodes", s).wait_recv()
        return c

    lax.fori_loop(1, peers, recv_r, 0)
    zbuf[mz] = jnp.sum(rbuf[...].astype(F32), axis=0).astype(BF16)

    def copy_z(p):
        return copy(zbuf.at[mz], zbuf.at[mz], s_z.at[p], r_z.at[mz], "events", p)

    def send_z(i, c):
        copy_z(lax.rem(mz + i, zs)).start()
        return c

    lax.fori_loop(1, zs, send_z, 0)

    def tiles_s(s):
        for k in range(slots):
            st2[s, k] = dot(ps[s, k], ret[s, k])

    tiles_s(me)

    def recv_b(i, c):
        s = lax.rem(me + peers - i, peers)
        copy(g1.at[s], ret.at[s], s_b.at[s], r_b.at[s], "nodes", s).wait_recv()
        tiles_s(s)
        return c

    lax.fori_loop(1, peers, recv_b, 0)

    def recv_z(i, c):
        s = lax.rem(mz + i, zs)
        copy(zbuf.at[s], zbuf.at[s], s_z.at[s], r_z.at[s], "events", s).wait_recv()
        return c

    lax.fori_loop(1, zs, recv_z, 0)
    abuf[me] = (jnp.sum(zbuf[...].astype(F32), axis=0) * scale).astype(BF16)

    def copy_g(p):
        return copy(abuf.at[me], abuf.at[me], s_g.at[p], r_g.at[me], "nodes", p)

    def send_g(i, c):
        copy_g(lax.rem(me + i, peers)).start()
        return c

    lax.fori_loop(1, peers, send_g, 0)

    def final(c, carry):
        at = pl.ds(pl.multiple_of(c * span, span), span)
        ss = jnp.concatenate(
            [spread(st2, sblk, c * group + j).astype(BF16) for j in range(group)], axis=0
        )
        total = (
            cot[0, at, :].astype(F32)
            + dot_tr(g2[at, :], wn1[:width, :])
            + dot_tr(sd[at, :], w1[width : 2 * width, :])
            + dot_tr(ss, w1[:width, :])
        )
        ngrad[0, at, :] = total.astype(BF16)
        return carry

    lax.fori_loop(0, nblk // group, final, 0)

    def recv_g(i, c):
        s = lax.rem(me + i, peers)
        copy(abuf.at[s], abuf.at[s], s_g.at[s], r_g.at[s], "nodes", s).wait_recv()
        return c

    lax.fori_loop(1, peers, recv_g, 0)
    grads[...] = abuf[...].reshape(peers * chunk, width)

    def drain(i, c):
        p = lax.rem(me + i, peers)
        copy_a(p).wait_send()
        copy_b(p).wait_send()
        copy_r(p).wait_send()
        copy_g(p).wait_send()
        return c

    lax.fori_loop(1, peers, drain, 0)

    def drain_z(i, c):
        copy_z(lax.rem(mz + i, zs)).wait_send()
        return c

    lax.fori_loop(1, zs, drain_z, 0)


def shards(
    peers,
    zs,
    nodes_in,
    edge_latents,
    src_block,
    src_offset,
    dst_block,
    dst_offset,
    tile_counts,
    w_edge1,
    b_edge1,
    w_edge2,
    b_edge2,
    w_node1,
    b_node1,
    w_node2,
    b_node2,
    cotangent,
):
    rows, width = nodes_in.shape[1:]
    slots, tile = src_offset.shape[3:]
    scale = float(zs * peers * rows) ** (-0.5)
    need = 7 * width + 16
    chunk = -(-need // (16 * peers)) * 16
    vec = lambda v: v.reshape(1, -1)
    vm = pl.BlockSpec(memory_space=pltpu.VMEM)
    hbm = pl.BlockSpec(memory_space=pl.ANY)
    sm = pl.BlockSpec(memory_space=pltpu.SMEM)
    tiles = (peers, slots, tile, width)
    sds = jax.ShapeDtypeStruct
    dma = pltpu.SemaphoreType.DMA
    args = (
        nodes_in.reshape(1, rows // tile, tile, width),
        edge_latents,
        src_block,
        src_offset,
        dst_block,
        dst_offset,
        tile_counts,
        w_edge1,
        vec(b_edge1),
        w_edge2,
        vec(b_edge2),
        w_node1,
        vec(b_node1),
        w_node2,
        vec(b_node2),
        cotangent,
    )
    held = (3, 0, 5, 1, 7, 8, 15, 9, 10, 11, 12, 13, 14)
    outs = pl.pallas_call(
        functools.partial(staged, peers, zs, scale, held),
        out_shape=(
            sds((1, rows, width), BF16),
            sds((1, rows, width), BF16),
            sds((peers * chunk, width), BF16),
        ),
        in_specs=[sm if j in (2, 4, 6) else hbm for j in range(16)],
        out_specs=(vm,) * 3,
        scratch_shapes=[
            pltpu.VMEM(tiles, BF16),
            pltpu.VMEM(tiles, BF16),
            pltpu.VMEM((peers, slots, tile, tile), BF16),
            pltpu.VMEM((peers, slots, tile, tile), BF16),
            pltpu.VMEM(tiles, BF16),
            pltpu.VMEM(tiles, F32),
            pltpu.VMEM(tiles, BF16),
            pltpu.VMEM(tiles, BF16),
            pltpu.VMEM(tiles, BF16),
            pltpu.VMEM(tiles, BF16),
            pltpu.VMEM(tiles, F32),
            pltpu.VMEM(tiles, F32),
            pltpu.VMEM((rows, width), F32),
            pltpu.VMEM((rows, width), BF16),
            pltpu.VMEM((rows, width), BF16),
            pltpu.VMEM((rows, width), BF16),
            pltpu.VMEM((rows // tile, tile, width), BF16),
            pltpu.VMEM((rows, width), BF16),
            pltpu.VMEM((peers * chunk, width), BF16),
            pltpu.VMEM((peers, chunk, width), BF16),
            pltpu.VMEM((zs, chunk, width), BF16),
            pltpu.VMEM((peers, chunk, width), BF16),
        ]
        + [dma((peers,))] * 6
        + [dma((zs,))] * 2
        + [dma((peers,))] * 2
        + [pltpu.VMEM(args[j].shape, args[j].dtype) for j in held]
        + [dma((len(held),))],
        compiler_params=pltpu.CompilerParams(
            collective_id=0, has_side_effects=True, vmem_limit_bytes=56 * 1024 * 1024
        ),
    )(*args)
    upd, ngrad, grads = outs
    grads = grads.astype(F32)
    cut = lambda i, j: grads[i * width : j * width]
    line = lambda i: grads[7 * width + i]
    return (
        upd,
        ngrad,
        cut(0, 3),
        line(0),
        cut(3, 4),
        line(1),
        cut(4, 6),
        line(2),
        cut(6, 7),
        line(3),
    )


def solution(mesh):
    return jax.shard_map(
        functools.partial(shards, mesh.shape["nodes"], mesh.shape["events"]),
        mesh=mesh,
        in_specs=(
            P("events", "nodes", None),
            P("events", "nodes", None, None, None, None),
            P("events", "nodes", None, None),
            P("events", "nodes", None, None, None),
            P("events", "nodes", None, None),
            P("events", "nodes", None, None, None),
            P("events", None, None),
            P(),
            P(),
            P(),
            P(),
            P(),
            P(),
            P(),
            P(),
            P("events", "nodes", None),
        ),
        out_specs=(
            P("events", "nodes", None),
            P("events", "nodes", None),
            P(),
            P(),
            P(),
            P(),
            P(),
            P(),
            P(),
            P(),
        ),
        check_vma=False,
    )
```
